128 devices in a mesh: fsdp: 8 (over z, core), dp: 16 (over y, x).
Axes of the slice: x: 4, y: 4, z: 4, core: 2. Of those that a mesh axis runs over, the one named last changes fastest.
Arguments:
- activations: bfloat16 [2048, 4096], P('dp', 'fsdp'), may hold values from -6 to 6
- out_grads: bfloat16 [2048, 16, 1024], P('dp', 'fsdp'), may hold values from -0.0390625 to 0.0390625
- owners: int32 [8, 16, 1], P('fsdp'), may hold values from 0 to 15; in each aligned block of 16 rows (0 to 15, 16 to 31, ..., all dimensions but the last counted through in order) at most 2 rows name the same one
- left_stats: bfloat16 [8, 32, 1024, 1024], P('fsdp', 'dp'), may hold values from -1 to 2, as said below
- right_stats: bfloat16 [8, 32, 512, 512], P('fsdp', 'dp'), may hold values from -1 to 2, as said below
- left_roots: bfloat16 [8, 32, 1024, 1024], P('fsdp', 'dp'), may hold values from -1 to 1, as said below
- right_roots: bfloat16 [8, 32, 512, 512], P('fsdp', 'dp'), may hold values from -1 to 1, as said below
Outputs:
- new_left_stats: bfloat16 [8, 32, 1024, 1024], P('fsdp', 'dp')
- new_right_stats: bfloat16 [8, 32, 512, 512], P('fsdp', 'dp')
- new_left_roots: bfloat16 [8, 32, 1024, 1024], P('fsdp', 'dp')
- new_right_roots: bfloat16 [8, 32, 512, 512], P('fsdp', 'dp')
- direction: bfloat16 [16, 1024, 4096], P(None, 'dp', 'fsdp')
The draws below stay inside these ranges and needn't reach their ends.
Inputs may be any that keep to these rules, and one draw needn't show every extreme that they name: `owners`: within each of the 8 rows no value appears more than 2 times, and in some row one value appears exactly 2 times. `left_stats`: each matrix is symmetric and each diagonal entry exceeds the sum of the magnitudes of the other entries of its row. `right_stats`: each matrix is symmetric and each diagonal entry exceeds the sum of the magnitudes of the other entries of its row. `left_roots`: each matrix is symmetric. `right_roots`: each matrix is symmetric.
All inputs are finite; a program needn't handle non-finite values.
Results may differ from the reference program's by a relative error of at most 0.022.
Values may be sent and summed in bfloat16 or wider, within the bound.
No kernel may reach another device: no remote copies, remote signals or barrier semaphores. Data moves between devices by JAX's collectives and lax.ppermute only.
A program may use at most 128 MiB of HBM per device.

```python
import math
import jax
import jax.numpy as jnp
import numpy as np
from jax import lax

DW = 4096
BS = 1024
MOST = 2
TOK_DEV = 128
TOKENS = 2048
BC = 512
NR = 16
N_FSDP = 8
N_DP = 16


def assemble_stats(diagonal, raw):
    order = raw.shape[-1]
    symmetric = 0.5 * (raw + jnp.swapaxes(raw, -1, -2)) * (0.25 / (order - 1))
    identity = jnp.eye(order, dtype=jnp.float32)
    return symmetric * (1.0 - identity) + diagonal[..., None] * identity


def assemble_root(diagonal, raw):
    order = raw.shape[-1]
    symmetric = 0.5 * (raw + jnp.swapaxes(raw, -1, -2)) * (0.21 / order ** 0.5)
    identity = jnp.eye(order, dtype=jnp.float32)
    return symmetric * (1.0 - identity) + diagonal[..., None] * identity


def draw_left_stats(key, part):
    key = jax.random.fold_in(key, 11)
    diag_key, noise_key = jax.random.split(key)
    leading = (N_FSDP, N_DP * MOST, BS)
    diagonal = jnp.exp(jax.random.uniform(diag_key, leading, jnp.float32, -0.6931, 0.6931))
    raw = jnp.clip(jax.random.normal(noise_key, leading + (BS,), jnp.float32) * 0.5, -1.0, 1.0)
    return assemble_stats(diagonal, raw).astype(jnp.bfloat16)


def draw_right_stats(key, part):
    key = jax.random.fold_in(key, 12)
    diag_key, noise_key = jax.random.split(key)
    leading = (N_FSDP, N_DP * MOST, BC)
    diagonal = jnp.exp(jax.random.uniform(diag_key, leading, jnp.float32, -0.6931, 0.6931))
    raw = jnp.clip(jax.random.normal(noise_key, leading + (BC,), jnp.float32) * 0.5, -1.0, 1.0)
    return assemble_stats(diagonal, raw).astype(jnp.bfloat16)


def draw_left_roots(key, part):
    key = jax.random.fold_in(key, 13)
    diag_key, noise_key = jax.random.split(key)
    leading = (N_FSDP, N_DP * MOST, BS)
    diagonal = 0.75 * (1.0 + 0.1 * jax.random.normal(diag_key, leading, jnp.float32).clip(-1.0, 1.0))
    raw = jnp.clip(jax.random.normal(noise_key, leading + (BS,), jnp.float32), -3.0, 3.0)
    return assemble_root(diagonal, raw).astype(jnp.bfloat16)


def draw_right_roots(key, part):
    key = jax.random.fold_in(key, 14)
    diag_key, noise_key = jax.random.split(key)
    leading = (N_FSDP, N_DP * MOST, BC)
    diagonal = 0.75 * (1.0 + 0.1 * jax.random.normal(diag_key, leading, jnp.float32).clip(-1.0, 1.0))
    raw = jnp.clip(jax.random.normal(noise_key, leading + (BC,), jnp.float32), -3.0, 3.0)
    return assemble_root(diagonal, raw).astype(jnp.bfloat16)


def strengthened(array, stream_key, source, target, parts, factor):
    owner, partner = [(jnp.arange(array.shape[position]) // (array.shape[position] // parts)).reshape([-1 if axis == position else 1 for axis in range(array.ndim)]) for position in (source, target)]
    chosen = jax.random.permutation(stream_key, parts)[partner]
    strong = (owner == chosen) | (owner == (partner + parts // 2) % parts)
    return jnp.where(strong, factor * array, array)


def block_scale(stream_key, shape, pieces, low, top_value):
    def one(dim, blocks):
        steps = jax.random.uniform(jax.random.fold_in(jax.random.fold_in(stream_key, 6), dim), (blocks,), jnp.float32, low / len(pieces), top_value / len(pieces))
        return jnp.repeat(jnp.exp(steps), shape[dim] // blocks).reshape((-1,) + (1,) * (len(shape) - dim - 1))

    gain = one(*pieces[0])
    for cut in pieces[1:]:
        gain = gain * one(*cut)
    return gain


def assign_block(stream_key, own, number, rows, amount, top, limit, lean):
    ranking = jax.random.permutation(stream_key, amount)
    packed, common = load_shares(amount, rows * top, limit, lean, True), load_shares(amount, rows * top, limit, lean, False)
    places = jnp.arange(amount)

    def named(sizes, rotation):
        used = int((sizes > 0).sum())
        fixed = max(1, used // 4)
        shifted = fixed + (places - fixed + rotation * (used - fixed)) % max(1, amount - fixed)
        return jnp.zeros((amount,), jnp.int32).at[ranking[jnp.where(places < fixed, places, shifted)]].set(jnp.asarray(sizes, jnp.int32))

    sizes = jnp.where(number % 4 == 0, named(packed, number // 4), named(common, number - number // 4 - 1))
    mixed = jax.random.permutation(jax.random.fold_in(own, 3), amount)
    giver, sink = mixed[0:amount // 2 * 2:2], mixed[1:amount // 2 * 2:2]
    slack = jnp.minimum(sizes[giver] - 1, limit - sizes[sink]) // 2
    slack = jnp.where((giver == ranking[0]) | (sink == ranking[0]) | (sizes[sink] == 0), 0, jnp.maximum(slack, 0))
    shifted = jax.random.randint(jax.random.fold_in(own, 4), (amount // 2,), 0, 1 << 20) % (slack + 1)
    sizes = sizes.at[giver].add(-shifted).at[sink].add(shifted)
    items = jnp.searchsorted(jnp.cumsum(sizes), jnp.arange(rows * top), side="right").astype(jnp.int32)
    grid = items.reshape(top, rows).T
    grid = grid[jax.random.permutation(jax.random.fold_in(own, 1), rows)]
    rotation = jax.random.randint(jax.random.fold_in(own, 2), (rows, 1), 0, top)
    return jnp.take_along_axis(grid, (jnp.arange(top)[None, :] + rotation) % top, axis=1)


def load_shares(amount, total, reach, skew, full):
    loads = [(1 << 20) // math.isqrt(rank ** skew) + 1 for rank in range(1, amount + 1)]
    largest = reach if full else min(reach, max(-(-total // amount), total * loads[0] // sum(loads)))
    least = 1 if total - largest >= amount - 1 else 0
    holding, spare = [largest] + [least] * (amount - 1), total - largest - least * (amount - 1)
    while spare > 0:
        free = [i for i in range(1, amount) if holding[i] < largest] or [i for i in range(1, amount) if holding[i] < reach]
        whole, left = sum([loads[i] for i in free]), spare
        for i in free:
            more = min(reach - holding[i], max(1, left * loads[i] // whole), spare)
            holding[i] = holding[i] + more
            spare = spare - more
    return np.array(holding)


def scatter_about(key, dims, spread, most, pieces=(), kind=jnp.bfloat16):
    factor_of = block_scale(key, dims, pieces, -0.22, 0.18) if pieces else 1.0
    array = jax.random.normal(key, dims, jnp.float32) * spread * factor_of
    return jnp.minimum(jnp.maximum(array, -most), most).astype(kind)


def gaussian_with(key, extent, spread, most, cuts, heavy, kind=jnp.bfloat16):
    values = spread * jax.random.normal(key, extent, jnp.float32)
    if cuts:
        values = values * block_scale(key, extent, cuts, -0.22, 0.18)
    return jnp.clip(strengthened(values, jax.random.fold_in(key, 3), *heavy), -most, most).astype(kind)


def setup_inputs(seed: int = 0) -> dict:
    streams_of = jax.random.split(jax.random.key(seed), 8)
    activations = scatter_about(streams_of[0], (TOKENS, DW), 1.0, 6.0, ((0, 16), (1, 8)))
    out_grads = gaussian_with(streams_of[1], (TOKENS, NR, BS), (TOK_DEV * N_DP * 25) ** -0.5, 0.0390625, ((0, 16), (1, 8)), (0, 2, 16, 2.0))
    owners_keys = jax.random.split(jax.random.fold_in(streams_of[2], 1), N_FSDP * NR // NR)
    owners_turns = jax.random.permutation(jax.random.fold_in(streams_of[2], 3), N_FSDP * NR // NR)
    owners = jax.vmap(lambda own, number: assign_block(jax.random.fold_in(streams_of[2], 2), own, number, NR, N_DP, 1, MOST, 2))(owners_keys, owners_turns).reshape((N_FSDP, NR, 1))
    left_stats = draw_left_stats(jax.random.fold_in(streams_of[7], 71), 0)
    right_stats = draw_right_stats(jax.random.fold_in(streams_of[7], 71), 0)
    left_roots = draw_left_roots(jax.random.fold_in(streams_of[7], 71), 0)
    right_roots = draw_right_roots(jax.random.fold_in(streams_of[7], 71), 0)
    return dict(activations=activations, out_grads=out_grads, owners=owners, left_stats=left_stats, right_stats=right_stats, left_roots=left_roots, right_roots=right_roots)


DECAY_RATE = 0.95


def newton_root(prev_root, factor):
    square = jnp.dot(prev_root, prev_root, preferred_element_type=jnp.float32).astype(jnp.bfloat16)
    fourth = jnp.dot(square, square, preferred_element_type=jnp.float32).astype(jnp.bfloat16)
    moment = jnp.dot(fourth, factor, preferred_element_type=jnp.float32)
    identity = jnp.eye(factor.shape[0], dtype=jnp.float32)
    newton_step = ((5.0 * identity - moment) * 0.25).astype(jnp.bfloat16)
    return jnp.dot(prev_root, newton_step, preferred_element_type=jnp.float32).astype(jnp.bfloat16)


def gram_rows(block):
    return lax.dot_general(block, block, (((1,), (1,)), ((), ())), preferred_element_type=jnp.float32)


def gram_cols(block):
    return lax.dot_general(block, block, (((0,), (0,)), ((), ())), preferred_element_type=jnp.float32)


def slot_ranks(owner_row):
    positions = jnp.arange(owner_row.shape[0])
    same_owner = owner_row[:, None] == owner_row[None, :]
    earlier = positions[None, :] < positions[:, None]
    return jnp.sum(jnp.where(same_owner & earlier, 1, 0), axis=1).astype(jnp.int32)


def reference(activations, out_grads, owners, left_stats, right_stats, left_roots, right_roots):
    grads_split = out_grads.reshape(N_DP, TOK_DEV, NR, BS)
    acts_split = activations.reshape(N_DP, TOK_DEV, N_FSDP, BC)
    owner_table = owners[:, :, 0].astype(jnp.int32)
    rank_table = jax.vmap(slot_ranks)(owner_table)
    direction_init = jnp.zeros((NR, BS, DW), jnp.bfloat16)

    def one_block(block_index, state_tuple):
        left_out, right_out, lroot_out, rroot_out, direction = state_tuple
        fsdp_index = (block_index // NR).astype(jnp.int32)
        row_index = (block_index % NR).astype(jnp.int32)
        grad_piece = lax.dynamic_index_in_dim(grads_split, row_index, 2, keepdims=False)
        acts_piece = lax.dynamic_index_in_dim(acts_split, fsdp_index, 2, keepdims=False)
        partial_value = jnp.einsum("jtb,jtc->jbc", grad_piece.astype(jnp.float32), acts_piece.astype(jnp.float32)).astype(jnp.bfloat16)
        grad_block = jnp.sum(partial_value.astype(jnp.float32), axis=0).astype(jnp.bfloat16)
        slot_index = (owner_table[fsdp_index, row_index] * MOST + rank_table[fsdp_index, row_index]).astype(jnp.int32)
        left_prev = left_stats[fsdp_index, slot_index]
        right_prev = right_stats[fsdp_index, slot_index]
        left_root = left_roots[fsdp_index, slot_index]
        right_root = right_roots[fsdp_index, slot_index]
        left_new = (DECAY_RATE * left_prev.astype(jnp.float32) + (1.0 - DECAY_RATE) * gram_rows(grad_block)).astype(jnp.bfloat16)
        right_new = (DECAY_RATE * right_prev.astype(jnp.float32) + (1.0 - DECAY_RATE) * gram_cols(grad_block)).astype(jnp.bfloat16)
        left_next = newton_root(left_root, left_new)
        right_next = newton_root(right_root, right_new)
        half_done = jnp.dot(left_root, grad_block, preferred_element_type=jnp.float32).astype(jnp.bfloat16)
        result_block = jnp.dot(half_done, right_root, preferred_element_type=jnp.float32).astype(jnp.bfloat16)
        left_out = left_out.at[fsdp_index, slot_index].set(left_new)
        right_out = right_out.at[fsdp_index, slot_index].set(right_new)
        lroot_out = lroot_out.at[fsdp_index, slot_index].set(left_next)
        rroot_out = rroot_out.at[fsdp_index, slot_index].set(right_next)
        anchor = (row_index, jnp.zeros((), jnp.int32), (fsdp_index * BC).astype(jnp.int32))
        direction = lax.dynamic_update_slice(direction, result_block[None], anchor)
        return (left_out, right_out, lroot_out, rroot_out, direction)

    outcome = lax.fori_loop(0, N_FSDP * NR, one_block, (left_stats, right_stats, left_roots, right_roots, direction_init))
    return (outcome[0], outcome[1], outcome[2], outcome[3], outcome[4])
```

```python
import functools

import jax
import jax.numpy as jnp
from jax import lax
from jax.experimental import pallas as pl
from jax.experimental.pallas import tpu as pltpu
from jax.sharding import Mesh
from jax.sharding import PartitionSpec as P

DECAY_RATE = 0.95
DP = ("y", "x")
FSDP = ("z", "c")
CHUNK = 256
MIB = 1 << 20


def dot(a, b):
    return jnp.dot(a, b, preferred_element_type=jnp.float32)


def params(mib):
    return pltpu.CompilerParams(vmem_limit_bytes=mib * MIB)


def cost(flops, nbytes):
    return pl.CostEstimate(flops=flops, bytes_accessed=nbytes, transcendentals=0)


def rows_loop(total, fn):
    step = min(CHUNK, total)
    for start in range(0, total, step):
        fn(pl.ds(start, step), start)


def powers_kernel(count, left, right, left4, right4, left2, right2):
    @pl.when(pl.program_id(0) < count[0])
    def _():
        for x, sq, out in ((left, left2, left4), (right, right2, right4)):
            order = x.shape[1]

            def square(rows, _, x=x, sq=sq):
                sq[rows] = dot(x[0, rows], x[0]).astype(jnp.bfloat16)

            def fourth(rows, _, sq=sq, out=out):
                out[0, rows] = dot(sq[rows], sq[...]).astype(jnp.bfloat16)

            rows_loop(order, square)
            rows_loop(order, fourth)


def root_powers(count, left, right):
    slots, nl, _ = left.shape
    nr = right.shape[1]
    spec = lambda n: pl.BlockSpec((1, n, n), lambda m, c: (m, 0, 0))
    return pl.pallas_call(
        powers_kernel,
        grid_spec=pltpu.PrefetchScalarGridSpec(
            num_scalar_prefetch=1,
            grid=(slots,),
            in_specs=[spec(nl), spec(nr)],
            out_specs=[spec(nl), spec(nr)],
            scratch_shapes=[pltpu.VMEM((nl, nl), jnp.bfloat16), pltpu.VMEM((nr, nr), jnp.bfloat16)],
        ),
        out_shape=[
            jax.ShapeDtypeStruct(left.shape, jnp.bfloat16),
            jax.ShapeDtypeStruct(right.shape, jnp.bfloat16),
        ],
        compiler_params=params(32),
        cost_estimate=cost(slots * 4 * (nl**3 + nr**3), slots * 4 * (nl**2 + nr**2)),
        name="root_powers",
    )(count, left, right)


def strips_kernel(where, first, acts, *refs):
    planes, out = refs[:-1], refs[-1]
    strip = out.shape[1]
    groups = []
    for z in range(3):
        groups.append(((planes[2 * z],), (planes[2 * z + 1],)))
    groups.append((planes[6:8], planes[8:10]))
    for z, group in enumerate(groups):
        rows = [
            jnp.concatenate([ref[s] for ref in refs_of for s in range(ref.shape[0])], axis=1)
            for refs_of in group
        ]
        g = dot(jnp.concatenate(rows, axis=0), acts[...]).astype(jnp.bfloat16)
        for k in range(2):
            for q in range(2):
                r = first[2 * z + k] + q
                out[where[r]] = g[(2 * k + q) * strip : (2 * k + q + 1) * strip]


def grad_strips(where, first, acts, planes, n_slots, strip):
    tokens, cols = acts.shape
    vmem = pl.BlockSpec(memory_space=pltpu.VMEM)
    smem = pl.BlockSpec(memory_space=pltpu.SMEM)
    rows = sum(p.size for p in planes) // tokens
    return pl.pallas_call(
        strips_kernel,
        in_specs=[smem] * 2 + [vmem] * (1 + len(planes)),
        out_specs=vmem,
        out_shape=jax.ShapeDtypeStruct((n_slots, strip, cols), jnp.bfloat16),
        compiler_params=params(32),
        cost_estimate=cost(2 * rows * tokens * cols, 2 * (rows * tokens + tokens * cols + rows * cols)),
        name="grad_strips",
    )(where, first, acts, *planes)


def direction_kernel(count, grads, left, right, out, half):
    @pl.when(pl.program_id(0) < count[0])
    def _():
        n, cols = left.shape[1], right.shape[1]
        strip = grads.shape[2]
        per = CHUNK // strip
        g = grads[:, 0].reshape(n, cols)

        def rows_of(rows, _):
            half[rows] = dot(left[0, rows], g).astype(jnp.bfloat16)

        rows_loop(n, rows_of)

        for i in range(n // CHUNK):
            d = dot(half[pl.ds(i * CHUNK, CHUNK)], right[0]).astype(jnp.bfloat16)
            out[pl.ds(i * per, per), 0] = d.reshape(per, strip, cols)


def directions(count, grads, left, right):
    replicas, slots, strip, cols = grads.shape
    n = left.shape[1]
    gspec = pl.BlockSpec((replicas, 1, strip, cols), lambda m, c: (0, m, 0, 0))
    spec = lambda k: pl.BlockSpec((1, k, k), lambda m, c: (m, 0, 0))
    return pl.pallas_call(
        direction_kernel,
        grid_spec=pltpu.PrefetchScalarGridSpec(
            num_scalar_prefetch=1,
            grid=(slots,),
            in_specs=[gspec, spec(n), spec(cols)],
            out_specs=gspec,
            scratch_shapes=[pltpu.VMEM((n, cols), jnp.bfloat16)],
        ),
        out_shape=jax.ShapeDtypeStruct(grads.shape, jnp.bfloat16),
        compiler_params=params(32),
        cost_estimate=cost(slots * 2 * n * cols * (n + cols), slots * 2 * (n * n + cols * cols + 2 * n * cols)),
        name="directions",
    )(count, grads, left, right)


def newton(stats, factor4, root, new_stats, step, new_root, gram_rows, ready):
    order = root.shape[0]

    def one_stats(rows, _):
        new_stats[rows] = (
            DECAY_RATE * stats[rows].astype(jnp.float32) + (1.0 - DECAY_RATE) * gram_rows(rows)
        ).astype(jnp.bfloat16)

    def one_step(rows, start):
        moment = dot(factor4[rows], new_stats[...])
        size = moment.shape[0]
        row = lax.broadcasted_iota(jnp.int32, (size, order), 0) + start
        col = lax.broadcasted_iota(jnp.int32, (size, order), 1)
        identity = jnp.where(row == col, 1.0, 0.0)
        step[rows] = ((5.0 * identity - moment) * 0.25).astype(jnp.bfloat16)

    def one_root(rows, _):
        new_root[rows] = dot(root[rows], step[...]).astype(jnp.bfloat16)

    ready(0)
    rows_loop(order, one_stats)
    ready(1)
    rows_loop(order, one_step)
    ready(2)
    rows_loop(order, one_root)


def update_kernel(count, grads, lstats, rstats, lroot, rroot, lfour, rfour, *refs):
    outs, (bl, br, g, ol, orr, lstep, rstep, turned, isems, osems) = refs[:4], refs[4:]
    slots, n = lstats.shape[:2]
    cols = rstats.shape[1]
    strip = grads.shape[2]
    ins = ((lstats, lfour, lroot), (rstats, rfour, rroot))
    held = (bl, br)
    made = (ol, orr)

    def arriving(m, side, i):
        return pltpu.make_async_copy(ins[side][i].at[m], held[side].at[m, i], isems.at[m, side, i])

    def leaving(m, side, i):
        return pltpu.make_async_copy(made[side].at[m, i], outs[2 * i + side].at[m], osems.at[m, side, i])

    def kept(m, side, i):
        return pltpu.make_async_copy(held[side].at[m, 2 * i], outs[2 * i + side].at[m], osems.at[m, side, i])

    def fetch(m):
        for i in range(3):
            for side in range(2):
                arriving(m, side, i).start()

    fetch(0)
    for m in range(slots):
        used = m < count[0]

        @pl.when(used)
        def _(m=m):
            g[...] = grads[:, m].reshape(n, cols)
            turned[...] = g[...].T
            if m + 1 < slots:
                arriving(m, 0, 0).wait()
                fetch(m + 1)

            def left_gram(rows):
                return lax.dot_general(
                    g[rows], g[...], (((1,), (1,)), ((), ())), preferred_element_type=jnp.float32
                )

            def right_gram(rows):
                return dot(turned[rows], g[...])

            for side, gram, step in ((0, left_gram, lstep), (1, right_gram, rstep)):
                stats, four, root = (held[side].at[m, i] for i in range(3))
                newton(
                    stats, four, root, made[side].at[m, 0], step, made[side].at[m, 1], gram,
                    lambda i, side=side: None if m + 1 < slots and (side, i) == (0, 0) else arriving(m, side, i).wait(),
                )
                leaving(m, side, 0).start()
                leaving(m, side, 1).start()

        @pl.when(jnp.logical_not(used))
        def _(m=m):
            for side in range(2):
                for i in range(3):
                    arriving(m, side, i).wait()
                for i in range(2):
                    kept(m, side, i).start()
            if m + 1 < slots:
                fetch(m + 1)

    for m in range(slots):
        for side in range(2):
            for i in range(2):
                leaving(m, side, i).wait()


def update_slots(count, grads, lstats, rstats, lroot, rroot, lfour, rfour):
    replicas, slots, strip, cols = grads.shape
    n = lstats.shape[1]
    smem, vmem, hbm = (pl.BlockSpec(memory_space=k) for k in (pltpu.SMEM, pltpu.VMEM, pl.ANY))
    shape = lambda a: jax.ShapeDtypeStruct(a.shape, jnp.bfloat16)
    return pl.pallas_call(
        update_kernel,
        in_specs=[smem, vmem] + [hbm] * 6,
        out_specs=[hbm] * 4,
        scratch_shapes=[
            pltpu.VMEM((slots, 3, n, n), jnp.bfloat16),
            pltpu.VMEM((slots, 3, cols, cols), jnp.bfloat16),
            pltpu.VMEM((n, cols), jnp.bfloat16),
            pltpu.VMEM((slots, 2, n, n), jnp.bfloat16),
            pltpu.VMEM((slots, 2, cols, cols), jnp.bfloat16),
            pltpu.VMEM((n, n), jnp.bfloat16),
            pltpu.VMEM((cols, cols), jnp.bfloat16),
            pltpu.VMEM((cols, n), jnp.bfloat16),
            pltpu.SemaphoreType.DMA((slots, 2, 3)),
            pltpu.SemaphoreType.DMA((slots, 2, 2)),
        ],
        out_shape=[shape(lstats), shape(rstats), shape(lroot), shape(rroot)],
        compiler_params=params(56),
        cost_estimate=cost(
            slots * (2 * n * n * cols + 2 * n * cols * cols + 4 * (n**3 + cols**3)),
            slots * 2 * (5 * n * n + 5 * cols * cols + n * cols),
        ),
        name="update_slots",
    )(count, grads, lstats, rstats, lroot, rroot, lfour, rfour)


def pick_kernel(where, src, out):
    for r in range(out.shape[0]):
        out[r] = src[where[r]]


def pick(where, returned):
    blocks = where.shape[0]
    shape = (blocks,) + returned.shape[1:]
    vmem = pl.BlockSpec(memory_space=pltpu.VMEM)
    return pl.pallas_call(
        pick_kernel,
        in_specs=[pl.BlockSpec(memory_space=pltpu.SMEM), vmem],
        out_specs=vmem,
        out_shape=jax.ShapeDtypeStruct(shape, returned.dtype),
        compiler_params=params(16),
        cost_estimate=cost(0, 2 * 2 * returned.size),
        name="pick",
    )(where, returned)


def shift(value, axis, by):
    n = lax.axis_size(axis)
    return lax.ppermute(value, axis, [(i, (i + by) % n) for i in range(n)])


def swap_cores(value):
    return lax.ppermute(value, "c", [(0, 1), (1, 0)])


def ring_gather(value, axis):
    return [value] + [shift(value, axis, -k) for k in (1, 2, 3)]


def slot_ranks(owner_row):
    positions = jnp.arange(owner_row.shape[0])
    same_owner = owner_row[:, None] == owner_row[None, :]
    earlier = positions[None, :] < positions[:, None]
    return jnp.sum(jnp.where(same_owner & earlier, 1, 0), axis=1).astype(jnp.int32)


def body(activations, out_grads, owners, left_stats, right_stats, left_roots, right_roots):
    tokens, own_blocks, order = out_grads.shape
    replicas = lax.axis_size("y") * lax.axis_size("x")
    planes, cores = lax.axis_size("z"), lax.axis_size("c")
    strip = order // replicas
    slots = left_stats.shape[1]
    cols = activations.shape[1]

    owner_row = owners[0, :, 0]
    where = owner_row * slots + slot_ranks(owner_row)
    count = jnp.sum(jnp.where(owner_row == lax.axis_index(DP), 1, 0)).astype(jnp.int32).reshape(1)

    turned = out_grads.reshape(tokens, own_blocks, replicas, strip).transpose(2, 1, 3, 0)
    turned = turned.reshape(replicas, own_blocks * strip, tokens)
    own = lax.all_to_all(turned, DP, 0, 0, tiled=True)
    spread = jnp.broadcast_to(activations[None], (replicas,) + activations.shape)
    own, spread = lax.optimization_barrier((own, spread))
    acts = lax.all_to_all(spread, DP, 0, 0, tiled=True)

    down, up = shift(own, "z", 1), shift(own, "z", -1)
    own_too = swap_cores(own)
    h = replicas // 2
    far_lo, far_hi = shift(down[:h], "z", 1), shift(up[h:], "z", -1)
    down_too, up_too = swap_cores(down), swap_cores(up)
    far_lo_too, far_hi_too = swap_cores(far_lo), swap_cores(far_hi)
    pieces = [own, own_too, down, down_too, up, up_too, far_lo, far_hi, far_lo_too, far_hi_too]

    z, c = lax.axis_index("z"), lax.axis_index("c")
    zs = [z, (z + planes - 1) % planes, (z + 1) % planes, (z + 2) % planes]
    first = jnp.stack([(q * cores + k) * own_blocks for q in zs for k in (c, 1 - c)]).astype(jnp.int32)
    strips = grad_strips(where, first, acts.reshape(replicas * tokens, cols), pieces, replicas * slots, strip)
    arrived = lax.all_to_all(strips.reshape(replicas, slots, strip, cols), DP, 0, 0, tiled=True)
    lroots, rroots, _ = lax.optimization_barrier((left_roots[0], right_roots[0], strips))
    lfour, rfour = root_powers(count, lroots, rroots)
    arrived, lfour, rfour = lax.optimization_barrier((arrived, lfour, rfour))
    ready = directions(count, arrived, left_roots[0], right_roots[0])
    returned = lax.all_to_all(ready, DP, 0, 0, tiled=True)
    nls, nrs, nlr, nrr = update_slots(
        count, arrived, left_stats[0], right_stats[0], left_roots[0], right_roots[0], lfour, rfour
    )
    direction = pick(where, returned.reshape(replicas * slots, strip, cols))
    return nls[None], nrs[None], nlr[None], nrr[None], direction


def solution(mesh):
    fsdp, dp = mesh.shape["fsdp"], mesh.shape["dp"]
    torus = Mesh(mesh.devices.reshape(fsdp // 2, 2, dp // 4, 4), ("z", "c", "y", "x"))
    state = P(FSDP, DP, None, None)
    in_specs = (P(DP, FSDP), P(DP, FSDP, None), P(FSDP, None, None), state, state, state, state)
    out_specs = (state, state, state, state, P(None, DP, FSDP))
    return jax.shard_map(body, mesh=torus, in_specs=in_specs, out_specs=out_specs, check_vma=False)
```

```python
import functools

import jax
import jax.numpy as jnp
from jax import lax
from jax.experimental import pallas as pl
from jax.experimental.pallas import tpu as pltpu
from jax.sharding import Mesh
from jax.sharding import PartitionSpec as P

DECAY_RATE = 0.95
DP = ("y", "x")
FSDP = ("z", "c")
CHUNK = 256
WHOLE = 1024
GROUP = 2
MIB = 1 << 20


def dot(a, b):
    return jnp.dot(a, b, preferred_element_type=jnp.float32)


def params(mib):
    return pltpu.CompilerParams(vmem_limit_bytes=mib * MIB)


def in_hbm(*arrays):
    return [pltpu.with_memory_space_constraint(a, pltpu.HBM) for a in arrays]


def cost(flops, nbytes):
    return pl.CostEstimate(flops=flops, bytes_accessed=nbytes, transcendentals=0)


def rows_loop(total, fn):
    step = min(CHUNK, total)
    for start in range(0, total, step):
        fn(pl.ds(start, step), start)


def powers_kernel(count, left, right, left4, right4, lheld, rheld, lsq, rsq, lout, rout, isems, osems):
    sides = ((left, lheld, lsq, lout, left4), (right, rheld, rsq, rout, right4))

    def arriving(m, side):
        x, held = sides[side][:2]
        return pltpu.make_async_copy(x.at[m], held.at[m], isems.at[m, side])

    def leaving(m, side):
        return pltpu.make_async_copy(sides[side][3].at[m], sides[side][4].at[m], osems.at[m, side])

    for m in range(left.shape[0]):

        @pl.when(m < count[0])
        def _(m=m):
            for side in range(2):
                arriving(m, side).start()

    for m in range(left.shape[0]):

        @pl.when(m < count[0])
        def _(m=m):
            for side, (_, held, sq, out, _) in enumerate(sides):
                arriving(m, side).wait()

                def square(rows, _):
                    sq[rows] = dot(held[m, rows], held[m]).astype(jnp.bfloat16)

                def fourth(rows, _):
                    out[m, rows] = dot(sq[rows], sq[...]).astype(jnp.bfloat16)

                rows_loop(held.shape[1], square)
                rows_loop(held.shape[1], fourth)
                leaving(m, side).start()

    for m in range(left.shape[0]):

        @pl.when(m < count[0])
        def _(m=m):
            for side in range(2):
                leaving(m, side).wait()


def root_powers(count, left, right):
    slots, nl, _ = left.shape
    nr = right.shape[1]
    smem, hbm = pl.BlockSpec(memory_space=pltpu.SMEM), pl.BlockSpec(memory_space=pltpu.HBM)
    return pl.pallas_call(
        powers_kernel,
        in_specs=[smem, hbm, hbm],
        out_specs=[hbm, hbm],
        scratch_shapes=[
            pltpu.VMEM(left.shape, jnp.bfloat16),
            pltpu.VMEM(right.shape, jnp.bfloat16),
            pltpu.VMEM((nl, nl), jnp.bfloat16),
            pltpu.VMEM((nr, nr), jnp.bfloat16),
            pltpu.VMEM(left.shape, jnp.bfloat16),
            pltpu.VMEM(right.shape, jnp.bfloat16),
            pltpu.SemaphoreType.DMA((slots, 2)),
            pltpu.SemaphoreType.DMA((slots, 2)),
        ],
        out_shape=[pltpu.HBM(a.shape, jnp.bfloat16) for a in (left, right)],
        compiler_params=params(24),
        cost_estimate=cost(slots * 4 * (nl**3 + nr**3), slots * 4 * (nl**2 + nr**2)),
        name="root_powers",
    )(count, *in_hbm(left, right))


def strips_kernel(where, first, acts, *refs):
    planes, (out, held, sems) = refs[:-3], refs[-3:]
    strip = out.shape[1]

    groups = [((planes[2 * z],), (planes[2 * z + 1],)) for z in range(3)]
    groups.append((planes[6:8], planes[8:10]))
    copies = []
    for z in range(0, len(groups), GROUP):
        rows = [
            jnp.concatenate([ref[s] for ref in refs_of for s in range(ref.shape[0])], axis=1)
            for group in groups[z : z + GROUP]
            for refs_of in group
        ]
        g = dot(jnp.concatenate(rows, axis=0), acts[...]).astype(jnp.bfloat16)
        for k in range(2 * GROUP):
            for q in range(2):
                n = 4 * z + 2 * k + q
                held[n] = g[(2 * k + q) * strip : (2 * k + q + 1) * strip]
                copies.append(pltpu.make_async_copy(held.at[n], out.at[where[first[2 * z + k] + q]], sems.at[n]))
                copies[-1].start()
    for c in copies:
        c.wait()


def grad_strips(where, first, acts, planes, n_slots, strip):
    tokens, cols = acts.shape
    vmem = pl.BlockSpec(memory_space=pltpu.VMEM)
    smem = pl.BlockSpec(memory_space=pltpu.SMEM)
    rows = sum(p.size for p in planes) // tokens
    return pl.pallas_call(
        strips_kernel,
        in_specs=[smem] * 2 + [vmem] * (1 + len(planes)),
        out_specs=pl.BlockSpec(memory_space=pltpu.HBM),
        out_shape=pltpu.HBM((n_slots, strip, cols), jnp.bfloat16),
        scratch_shapes=[
            pltpu.VMEM((rows // strip, strip, cols), jnp.bfloat16),
            pltpu.SemaphoreType.DMA((rows // strip,)),
        ],
        compiler_params=params(32),
        cost_estimate=cost(2 * rows * tokens * cols, 2 * (rows * tokens + tokens * cols + rows * cols)),
        name="grad_strips",
    )(where, first, acts, *planes)


def direction_kernel(count, grads, left, right, out, lroot, rroot, half, done, lsem, rsem, osem):
    slots, n = left.shape[:2]
    cols = right.shape[1]
    strip = grads.shape[2]
    per = WHOLE // strip
    pieces = range(n // WHOLE)

    def rows(m, i):
        part = pl.ds(i * WHOLE, WHOLE)
        return pltpu.make_async_copy(left.at[m, part], lroot.at[m, part], lsem.at[m, i])

    def side(m):
        return pltpu.make_async_copy(right.at[m], rroot.at[m], rsem.at[m])

    def leaving(m, i):
        part = pl.ds(i * per, per)
        return pltpu.make_async_copy(done.at[m, part], out.at[part, m], osem.at[m, i])

    def fetch(m):
        @pl.when(m < count[0])
        def _():
            side(m).start()
            for i in pieces:
                rows(m, i).start()

    fetch(0)
    for m in range(slots):

        @pl.when(m < count[0])
        def _(m=m):
            side(m).wait()
            if m + 1 < slots:
                fetch(m + 1)
            half[...] = dot(grads[:, m].reshape(n, cols), rroot[m]).astype(jnp.bfloat16)
            for i in pieces:
                rows(m, i).wait()
                d = dot(lroot[m, pl.ds(i * WHOLE, WHOLE)], half[...]).astype(jnp.bfloat16)
                done[m, pl.ds(i * per, per)] = d.reshape(per, strip, cols)
                leaving(m, i).start()

    for m in range(slots):

        @pl.when(m < count[0])
        def _(m=m):
            for i in pieces:
                leaving(m, i).wait()


def directions(count, grads, left, right):
    replicas, slots, strip, cols = grads.shape
    n = left.shape[1]
    smem, vmem, hbm = (pl.BlockSpec(memory_space=k) for k in (pltpu.SMEM, pltpu.VMEM, pltpu.HBM))
    return pl.pallas_call(
        direction_kernel,
        in_specs=[smem, vmem, hbm, hbm],
        out_specs=hbm,
        scratch_shapes=[
            pltpu.VMEM((slots, n, n), jnp.bfloat16),
            pltpu.VMEM((slots, cols, cols), jnp.bfloat16),
            pltpu.VMEM((n, cols), jnp.bfloat16),
            pltpu.VMEM((slots, replicas, strip, cols), jnp.bfloat16),
            pltpu.SemaphoreType.DMA((slots, n // WHOLE)),
            pltpu.SemaphoreType.DMA((slots,)),
            pltpu.SemaphoreType.DMA((slots, n // WHOLE)),
        ],
        out_shape=pltpu.HBM(grads.shape, jnp.bfloat16),
        compiler_params=params(24),
        cost_estimate=cost(slots * 2 * n * cols * (n + cols), slots * 2 * (n * n + cols * cols + 2 * n * cols)),
        name="directions",
    )(count, grads, *in_hbm(left, right))


def newton(stats, factor4, root, new_stats, step, new_root, gram_rows, ready):
    order = root.shape[0]

    def one_stats(rows, _):
        new_stats[rows] = (
            DECAY_RATE * stats[rows].astype(jnp.float32) + (1.0 - DECAY_RATE) * gram_rows(rows)
        ).astype(jnp.bfloat16)

    def one_step(rows, start):
        moment = dot(factor4[rows], new_stats[...])
        size = moment.shape[0]
        row = lax.broadcasted_iota(jnp.int32, (size, order), 0) + start
        col = lax.broadcasted_iota(jnp.int32, (size, order), 1)
        identity = jnp.where(row == col, 1.0, 0.0)
        step[rows] = ((5.0 * identity - moment) * 0.25).astype(jnp.bfloat16)

    def one_root(rows, _):
        new_root[rows] = dot(root[rows], step[...]).astype(jnp.bfloat16)

    ready(0)
    rows_loop(order, one_stats)
    ready(1)
    rows_loop(order, one_step)
    ready(2)
    rows_loop(order, one_root)


def update_kernel(count, grads, lstats, rstats, lroot, rroot, lfour, rfour, *refs):
    outs, (bl, br, g, ol, orr, lstep, rstep, turned, isems, osems, gsems) = refs[:4], refs[4:]
    slots, n = lstats.shape[:2]
    cols = rstats.shape[1]
    strip = grads.shape[2]
    ins = ((lstats, lfour, lroot), (rstats, rfour, rroot))
    held = (bl, br)
    made = (ol, orr)

    def arriving(m, side, i):
        return pltpu.make_async_copy(ins[side][i].at[m], held[side].at[m, i], isems.at[m, side, i])

    def leaving(m, side, i):
        return pltpu.make_async_copy(made[side].at[m, i], outs[2 * i + side].at[m], osems.at[m, side, i])

    def kept(m, side, i):
        return pltpu.make_async_copy(held[side].at[m, 2 * i], outs[2 * i + side].at[m], osems.at[m, side, i])

    def block(m):
        return pltpu.make_async_copy(grads.at[:, m], g.at[m], gsems.at[m])

    def fetch(m):
        block(m).start()
        for i in range(3):
            for side in range(2):
                arriving(m, side, i).start()

    fetch(0)
    for m in range(slots):
        used = m < count[0]

        @pl.when(used)
        def _(m=m):
            block(m).wait()
            whole = g[m].reshape(n, cols)
            turned[...] = whole.T
            if m + 1 < slots:
                arriving(m, 0, 0).wait()
                fetch(m + 1)

            def left_gram(rows):
                part = g[m, pl.ds(rows.start // strip, rows.size // strip)].reshape(rows.size, cols)
                return dot(part, turned[...])

            def right_gram(rows):
                return dot(turned[rows], g[m].reshape(n, cols))

            for side, gram, step in ((0, left_gram, lstep), (1, right_gram, rstep)):
                stats, four, root = (held[side].at[m, i] for i in range(3))
                newton(
                    stats, four, root, made[side].at[m, 0], step, made[side].at[m, 1], gram,
                    lambda i, side=side: None if m + 1 < slots and (side, i) == (0, 0) else arriving(m, side, i).wait(),
                )
                leaving(m, side, 0).start()
                leaving(m, side, 1).start()

        @pl.when(jnp.logical_not(used))
        def _(m=m):
            block(m).wait()
            for side in range(2):
                for i in range(3):
                    arriving(m, side, i).wait()
                for i in range(2):
                    kept(m, side, i).start()
            if m + 1 < slots:
                fetch(m + 1)

    for m in range(slots):
        for side in range(2):
            for i in range(2):
                leaving(m, side, i).wait()


def update_slots(count, grads, lstats, rstats, lroot, rroot, lfour, rfour):
    replicas, slots, strip, cols = grads.shape
    n = lstats.shape[1]
    smem, hbm = pl.BlockSpec(memory_space=pltpu.SMEM), pl.BlockSpec(memory_space=pltpu.HBM)
    shape = lambda a: pltpu.HBM(a.shape, jnp.bfloat16)
    return pl.pallas_call(
        update_kernel,
        in_specs=[smem] + [hbm] * 7,
        out_specs=[hbm] * 4,
        scratch_shapes=[
            pltpu.VMEM((slots, 3, n, n), jnp.bfloat16),
            pltpu.VMEM((slots, 3, cols, cols), jnp.bfloat16),
            pltpu.VMEM((slots, replicas, strip, cols), jnp.bfloat16),
            pltpu.VMEM((slots, 2, n, n), jnp.bfloat16),
            pltpu.VMEM((slots, 2, cols, cols), jnp.bfloat16),
            pltpu.VMEM((n, n), jnp.bfloat16),
            pltpu.VMEM((cols, cols), jnp.bfloat16),
            pltpu.VMEM((cols, n), jnp.bfloat16),
            pltpu.SemaphoreType.DMA((slots, 2, 3)),
            pltpu.SemaphoreType.DMA((slots, 2, 2)),
            pltpu.SemaphoreType.DMA((slots,)),
        ],
        out_shape=[shape(lstats), shape(rstats), shape(lroot), shape(rroot)],
        compiler_params=params(56),
        cost_estimate=cost(
            slots * (2 * n * n * cols + 2 * n * cols * cols + 4 * (n**3 + cols**3)),
            slots * 2 * (5 * n * n + 5 * cols * cols + n * cols),
        ),
        name="update_slots",
    )(count, *in_hbm(grads, lstats, rstats, lroot, rroot, lfour, rfour))


def pick_kernel(where, src, out, sems):
    copies = [pltpu.make_async_copy(src.at[where[r]], out.at[r], sems.at[r]) for r in range(out.shape[0])]
    for c in copies:
        c.start()
    for c in copies:
        c.wait()


def pick(where, returned):
    blocks = where.shape[0]
    shape = (blocks,) + returned.shape[1:]
    return pl.pallas_call(
        pick_kernel,
        in_specs=[pl.BlockSpec(memory_space=pltpu.SMEM), pl.BlockSpec(memory_space=pltpu.VMEM)],
        out_specs=pl.BlockSpec(memory_space=pltpu.HBM),
        out_shape=pltpu.HBM(shape, returned.dtype),
        scratch_shapes=[pltpu.SemaphoreType.DMA((blocks,))],
        compiler_params=params(16),
        cost_estimate=cost(0, 2 * 2 * returned.size),
        name="pick",
    )(where, returned)


def shift(value, axis, by):
    n = lax.axis_size(axis)
    return lax.ppermute(value, axis, [(i, (i + by) % n) for i in range(n)])


def swap_cores(value):
    return lax.ppermute(value, "c", [(0, 1), (1, 0)])


def ring_gather(value, axis):
    return [value] + [shift(value, axis, -k) for k in (1, 2, 3)]


def slot_ranks(owner_row):
    positions = jnp.arange(owner_row.shape[0])
    same_owner = owner_row[:, None] == owner_row[None, :]
    earlier = positions[None, :] < positions[:, None]
    return jnp.sum(jnp.where(same_owner & earlier, 1, 0), axis=1).astype(jnp.int32)


def body(activations, out_grads, owners, left_stats, right_stats, left_roots, right_roots):
    tokens, own_blocks, order = out_grads.shape
    replicas = lax.axis_size("y") * lax.axis_size("x")
    planes, cores = lax.axis_size("z"), lax.axis_size("c")
    strip = order // replicas
    slots = left_stats.shape[1]
    cols = activations.shape[1]

    owner_row = owners[0, :, 0]
    where = owner_row * slots + slot_ranks(owner_row)
    count = jnp.sum(jnp.where(owner_row == lax.axis_index(DP), 1, 0)).astype(jnp.int32).reshape(1)

    turned = out_grads.reshape(tokens, own_blocks, replicas, strip).transpose(2, 1, 3, 0)
    turned = turned.reshape(replicas, own_blocks * strip, tokens)
    own = lax.all_to_all(turned, DP, 0, 0, tiled=True)
    spread = jnp.broadcast_to(activations[None], (replicas,) + activations.shape)
    own, spread = lax.optimization_barrier((own, spread))
    acts = lax.all_to_all(spread, DP, 0, 0, tiled=True)

    down, up = shift(own, "z", 1), shift(own, "z", -1)
    own_too = swap_cores(own)
    h = replicas // 2
    far_lo, far_hi = shift(down[:h], "z", 1), shift(up[h:], "z", -1)
    down_too, up_too = swap_cores(down), swap_cores(up)
    far_lo_too, far_hi_too = swap_cores(far_lo), swap_cores(far_hi)
    pieces = [own, own_too, down, down_too, up, up_too, far_lo, far_hi, far_lo_too, far_hi_too]

    z, c = lax.axis_index("z"), lax.axis_index("c")
    zs = [z, (z + planes - 1) % planes, (z + 1) % planes, (z + 2) % planes]
    first = jnp.stack([(q * cores + k) * own_blocks for q in zs for k in (c, 1 - c)]).astype(jnp.int32)
    strips = grad_strips(where, first, acts.reshape(replicas * tokens, cols), pieces, replicas * slots, strip)
    arrived = lax.all_to_all(strips.reshape(replicas, slots, strip, cols), DP, 0, 0, tiled=True)
    lroots, rroots, _ = lax.optimization_barrier((left_roots[0], right_roots[0], strips))
    lfour, rfour = root_powers(count, lroots, rroots)
    arrived, lfour, rfour = lax.optimization_barrier((arrived, lfour, rfour))
    ready = directions(count, arrived, left_roots[0], right_roots[0])
    returned = lax.all_to_all(ready, DP, 0, 0, tiled=True)
    nls, nrs, nlr, nrr = update_slots(
        count, arrived, left_stats[0], right_stats[0], left_roots[0], right_roots[0], lfour, rfour
    )
    direction = pick(where, returned.reshape(replicas * slots, strip, cols))
    return nls[None], nrs[None], nlr[None], nrr[None], direction


def solution(mesh):
    fsdp, dp = mesh.shape["fsdp"], mesh.shape["dp"]
    torus = Mesh(mesh.devices.reshape(fsdp // 2, 2, dp // 4, 4), ("z", "c", "y", "x"))
    state = P(FSDP, DP, None, None)
    in_specs = (P(DP, FSDP), P(DP, FSDP, None), P(FSDP, None, None), state, state, state, state)
    out_specs = (state, state, state, state, P(None, DP, FSDP))
    return jax.shard_map(body, mesh=torus, in_specs=in_specs, out_specs=out_specs, check_vma=False)
```

```python
import functools

import jax
import jax.numpy as jnp
from jax import lax
from jax.experimental import pallas as pl
from jax.experimental.pallas import tpu as pltpu
from jax.sharding import Mesh
from jax.sharding import PartitionSpec as P

DECAY_RATE = 0.95
DP = ("y", "x")
FSDP = ("z", "c")
CHUNK = 256
WHOLE = 1024
SPREAD_FLOPS = 8 * 10**9
EARLY_SLOTS = 1
GROUP = 2
MIB = 1 << 20


def dot(a, b):
    return jnp.dot(a, b, preferred_element_type=jnp.float32)


def params(mib):
    return pltpu.CompilerParams(vmem_limit_bytes=mib * MIB)


def in_hbm(*arrays):
    return [pltpu.with_memory_space_constraint(a, pltpu.HBM) for a in arrays]


def cost(flops, nbytes):
    return pl.CostEstimate(flops=flops, bytes_accessed=nbytes, transcendentals=0)


def rows_loop(total, fn):
    step = min(CHUNK, total)
    for start in range(0, total, step):
        fn(pl.ds(start, step), start)


def powers_kernel(last, left, right, left4, right4, lheld, rheld, lsq, rsq, lout, rout, isems, osems):
    sides = ((left, lheld, lsq, lout, left4), (right, rheld, rsq, rout, right4))

    def arriving(m, side):
        x, held = sides[side][:2]
        return pltpu.make_async_copy(x.at[m], held.at[m], isems.at[m, side])

    def leaving(m, side):
        return pltpu.make_async_copy(sides[side][3].at[m], sides[side][4].at[m], osems.at[m, side])

    for m in range(left.shape[0]):

        @pl.when(m < last[0])
        def _(m=m):
            for side in range(2):
                arriving(m, side).start()

    for m in range(left.shape[0]):

        @pl.when(m < last[0])
        def _(m=m):
            for side, (_, held, sq, out, _) in enumerate(sides):
                arriving(m, side).wait()

                def square(rows, _):
                    sq[rows] = dot(held[m, rows], held[m]).astype(jnp.bfloat16)

                def fourth(rows, _):
                    out[m, rows] = dot(sq[rows], sq[...]).astype(jnp.bfloat16)

                rows_loop(held.shape[1], square)
                rows_loop(held.shape[1], fourth)
                leaving(m, side).start()

    for m in range(left.shape[0]):

        @pl.when(m < last[0])
        def _(m=m):
            for side in range(2):
                leaving(m, side).wait()


def root_powers(last, left, right):
    slots, nl, _ = left.shape
    nr = right.shape[1]
    smem, hbm = pl.BlockSpec(memory_space=pltpu.SMEM), pl.BlockSpec(memory_space=pltpu.HBM)
    return pl.pallas_call(
        powers_kernel,
        in_specs=[smem, hbm, hbm],
        out_specs=[hbm, hbm],
        scratch_shapes=[
            pltpu.VMEM(left.shape, jnp.bfloat16),
            pltpu.VMEM(right.shape, jnp.bfloat16),
            pltpu.VMEM((nl, nl), jnp.bfloat16),
            pltpu.VMEM((nr, nr), jnp.bfloat16),
            pltpu.VMEM(left.shape, jnp.bfloat16),
            pltpu.VMEM(right.shape, jnp.bfloat16),
            pltpu.SemaphoreType.DMA((slots, 2)),
            pltpu.SemaphoreType.DMA((slots, 2)),
        ],
        out_shape=[pltpu.HBM(a.shape, jnp.bfloat16) for a in (left, right)],
        compiler_params=params(24),
        cost_estimate=cost(slots * 4 * (nl**3 + nr**3), slots * 4 * (nl**2 + nr**2)),
        name="root_powers",
    )(last, *in_hbm(left, right))


def strips_kernel(where, first, acts, *refs):
    planes, (out, held, sems) = refs[:-3], refs[-3:]
    strip = out.shape[1]

    groups = [((planes[2 * z],), (planes[2 * z + 1],)) for z in range(3)]
    groups.append((planes[6:8], planes[8:10]))
    copies = []
    for z in range(0, len(groups), GROUP):
        rows = [
            jnp.concatenate([ref[s] for ref in refs_of for s in range(ref.shape[0])], axis=1)
            for group in groups[z : z + GROUP]
            for refs_of in group
        ]
        g = dot(jnp.concatenate(rows, axis=0), acts[...]).astype(jnp.bfloat16)
        for k in range(2 * GROUP):
            for q in range(2):
                n = 4 * z + 2 * k + q
                held[n] = g[(2 * k + q) * strip : (2 * k + q + 1) * strip]
                copies.append(pltpu.make_async_copy(held.at[n], out.at[where[first[2 * z + k] + q]], sems.at[n]))
                copies[-1].start()
    for c in copies:
        c.wait()


def grad_strips(where, first, acts, planes, n_slots, strip):
    tokens, cols = acts.shape
    vmem = pl.BlockSpec(memory_space=pltpu.VMEM)
    smem = pl.BlockSpec(memory_space=pltpu.SMEM)
    rows = sum(p.size for p in planes) // tokens
    return pl.pallas_call(
        strips_kernel,
        in_specs=[smem] * 2 + [vmem] * (1 + len(planes)),
        out_specs=pl.BlockSpec(memory_space=pltpu.HBM),
        out_shape=pltpu.HBM((n_slots, strip, cols), jnp.bfloat16),
        scratch_shapes=[
            pltpu.VMEM((rows // strip, strip, cols), jnp.bfloat16),
            pltpu.SemaphoreType.DMA((rows // strip,)),
        ],
        compiler_params=params(32),
        cost_estimate=cost(2 * rows * tokens * cols, 2 * (rows * tokens + tokens * cols + rows * cols)),
        name="grad_strips",
    )(where, first, acts, *planes)


def direction_kernel(count, grads, left, right, out, lroot, rroot, half, done, lsem, rsem, osem):
    slots, n = left.shape[:2]
    cols = right.shape[1]
    strip = grads.shape[2]
    per = WHOLE // strip
    pieces = range(n // WHOLE)

    def rows(m, i):
        part = pl.ds(i * WHOLE, WHOLE)
        return pltpu.make_async_copy(left.at[m, part], lroot.at[m, part], lsem.at[m, i])

    def side(m):
        return pltpu.make_async_copy(right.at[m], rroot.at[m], rsem.at[m])

    def leaving(m, i):
        part = pl.ds(i * per, per)
        return pltpu.make_async_copy(done.at[m, part], out.at[part, m], osem.at[m, i])

    def fetch(m):
        @pl.when(m < count[0])
        def _():
            side(m).start()
            for i in pieces:
                rows(m, i).start()

    fetch(0)
    for m in range(slots):

        @pl.when(m < count[0])
        def _(m=m):
            side(m).wait()
            if m + 1 < slots:
                fetch(m + 1)
            half[...] = dot(grads[:, m].reshape(n, cols), rroot[m]).astype(jnp.bfloat16)
            for i in pieces:
                rows(m, i).wait()
                d = dot(lroot[m, pl.ds(i * WHOLE, WHOLE)], half[...]).astype(jnp.bfloat16)
                done[m, pl.ds(i * per, per)] = d.reshape(per, strip, cols)
                leaving(m, i).start()

    for m in range(slots):

        @pl.when(m < count[0])
        def _(m=m):
            for i in pieces:
                leaving(m, i).wait()


def directions(count, grads, left, right):
    replicas, slots, strip, cols = grads.shape
    n = left.shape[1]
    smem, vmem, hbm = (pl.BlockSpec(memory_space=k) for k in (pltpu.SMEM, pltpu.VMEM, pltpu.HBM))
    return pl.pallas_call(
        direction_kernel,
        in_specs=[smem, vmem, hbm, hbm],
        out_specs=hbm,
        scratch_shapes=[
            pltpu.VMEM((slots, n, n), jnp.bfloat16),
            pltpu.VMEM((slots, cols, cols), jnp.bfloat16),
            pltpu.VMEM((n, cols), jnp.bfloat16),
            pltpu.VMEM((slots, replicas, strip, cols), jnp.bfloat16),
            pltpu.SemaphoreType.DMA((slots, n // WHOLE)),
            pltpu.SemaphoreType.DMA((slots,)),
            pltpu.SemaphoreType.DMA((slots, n // WHOLE)),
        ],
        out_shape=pltpu.HBM(grads.shape, jnp.bfloat16),
        compiler_params=params(24),
        cost_estimate=cost(slots * 2 * n * cols * (n + cols), slots * 2 * (n * n + cols * cols + 2 * n * cols)),
        name="directions",
    )(count, grads, *in_hbm(left, right))


def newton(stats, factor4, root, new_stats, step, new_root, gram_rows, ready):
    order = root.shape[0]

    def one_stats(rows, _):
        new_stats[rows] = (
            DECAY_RATE * stats[rows].astype(jnp.float32) + (1.0 - DECAY_RATE) * gram_rows(rows)
        ).astype(jnp.bfloat16)

    def one_step(rows, start):
        moment = dot(factor4[rows], new_stats[...])
        size = moment.shape[0]
        row = lax.broadcasted_iota(jnp.int32, (size, order), 0) + start
        col = lax.broadcasted_iota(jnp.int32, (size, order), 1)
        identity = jnp.where(row == col, 1.0, 0.0)
        step[rows] = ((5.0 * identity - moment) * 0.25).astype(jnp.bfloat16)

    def one_root(rows, _):
        new_root[rows] = dot(root[rows], step[...]).astype(jnp.bfloat16)

    ready(0)
    rows_loop(order, one_stats)
    ready(1)
    rows_loop(order, one_step)
    ready(2)
    rows_loop(order, one_root)


def update_kernel(count, grads, lstats, rstats, lroot, rroot, lfour, rfour, *refs):
    outs, (bl, br, g, ol, orr, lstep, rstep, turned, isems, osems, gsems) = refs[:4], refs[4:]
    slots, n = lstats.shape[:2]
    cols = rstats.shape[1]
    strip = grads.shape[2]
    ins = ((lstats, lfour, lroot), (rstats, rfour, rroot))
    held = (bl, br)
    made = (ol, orr)

    def arriving(m, side, i):
        return pltpu.make_async_copy(ins[side][i].at[m], held[side].at[m, i], isems.at[m, side, i])

    def leaving(m, side, i):
        return pltpu.make_async_copy(made[side].at[m, i], outs[2 * i + side].at[m], osems.at[m, side, i])

    def kept(m, side, i):
        return pltpu.make_async_copy(held[side].at[m, 2 * i], outs[2 * i + side].at[m], osems.at[m, side, i])

    def block(m):
        return pltpu.make_async_copy(grads.at[:, m], g.at[m], gsems.at[m])

    def fetch(m):
        block(m).start()
        for i in range(3):
            for side in range(2):
                arriving(m, side, i).start()

    fetch(0)
    for m in range(slots):
        used = m < count[0]

        @pl.when(used)
        def _(m=m):
            block(m).wait()
            whole = g[m].reshape(n, cols)
            turned[...] = whole.T
            if m + 1 < slots:
                arriving(m, 0, 0).wait()
                fetch(m + 1)

            def left_gram(rows):
                part = g[m, pl.ds(rows.start // strip, rows.size // strip)].reshape(rows.size, cols)
                return dot(part, turned[...])

            def right_gram(rows):
                return dot(turned[rows], g[m].reshape(n, cols))

            for side, gram, step in ((0, left_gram, lstep), (1, right_gram, rstep)):
                stats, four, root = (held[side].at[m, i] for i in range(3))
                newton(
                    stats, four, root, made[side].at[m, 0], step, made[side].at[m, 1], gram,
                    lambda i, side=side: None if m + 1 < slots and (side, i) == (0, 0) else arriving(m, side, i).wait(),
                )
                leaving(m, side, 0).start()
                leaving(m, side, 1).start()

        @pl.when(jnp.logical_not(used))
        def _(m=m):
            block(m).wait()
            for side in range(2):
                for i in range(3):
                    arriving(m, side, i).wait()
                for i in range(2):
                    kept(m, side, i).start()
            if m + 1 < slots:
                fetch(m + 1)

    for m in range(slots):
        for side in range(2):
            for i in range(2):
                leaving(m, side, i).wait()


def update_slots(count, grads, lstats, rstats, lroot, rroot, lfour, rfour):
    replicas, slots, strip, cols = grads.shape
    n = lstats.shape[1]
    smem, hbm = pl.BlockSpec(memory_space=pltpu.SMEM), pl.BlockSpec(memory_space=pltpu.HBM)
    shape = lambda a: pltpu.HBM(a.shape, jnp.bfloat16)
    return pl.pallas_call(
        update_kernel,
        in_specs=[smem] + [hbm] * 7,
        out_specs=[hbm] * 4,
        scratch_shapes=[
            pltpu.VMEM((slots, 3, n, n), jnp.bfloat16),
            pltpu.VMEM((slots, 3, cols, cols), jnp.bfloat16),
            pltpu.VMEM((slots, replicas, strip, cols), jnp.bfloat16),
            pltpu.VMEM((slots, 2, n, n), jnp.bfloat16),
            pltpu.VMEM((slots, 2, cols, cols), jnp.bfloat16),
            pltpu.VMEM((n, n), jnp.bfloat16),
            pltpu.VMEM((cols, cols), jnp.bfloat16),
            pltpu.VMEM((cols, n), jnp.bfloat16),
            pltpu.SemaphoreType.DMA((slots, 2, 3)),
            pltpu.SemaphoreType.DMA((slots, 2, 2)),
            pltpu.SemaphoreType.DMA((slots,)),
        ],
        out_shape=[shape(lstats), shape(rstats), shape(lroot), shape(rroot)],
        compiler_params=params(56),
        cost_estimate=cost(
            slots * (2 * n * n * cols + 2 * n * cols * cols + 4 * (n**3 + cols**3)),
            slots * 2 * (5 * n * n + 5 * cols * cols + n * cols),
        ),
        name="update_slots",
    )(count, *in_hbm(grads, lstats, rstats, lroot, rroot, lfour, rfour))


def pick_kernel(where, src, out, sems):
    copies = [pltpu.make_async_copy(src.at[where[r]], out.at[r], sems.at[r]) for r in range(out.shape[0])]
    for c in copies:
        c.start()
    for c in copies:
        c.wait()


def pick(where, returned):
    blocks = where.shape[0]
    shape = (blocks,) + returned.shape[1:]
    return pl.pallas_call(
        pick_kernel,
        in_specs=[pl.BlockSpec(memory_space=pltpu.SMEM), pl.BlockSpec(memory_space=pltpu.VMEM)],
        out_specs=pl.BlockSpec(memory_space=pltpu.HBM),
        out_shape=pltpu.HBM(shape, returned.dtype),
        scratch_shapes=[pltpu.SemaphoreType.DMA((blocks,))],
        compiler_params=params(16),
        cost_estimate=cost(0, 2 * 2 * returned.size),
        name="pick",
    )(where, returned)


def spread_kernel(src, out, sems):
    copies = [pltpu.make_async_copy(src, out.at[r], sems.at[r]) for r in range(out.shape[0])]
    for c in copies:
        c.start()
    for c in copies:
        c.wait()


def spread_rows(src, replicas):
    shape = (replicas,) + src.shape
    return pl.pallas_call(
        spread_kernel,
        in_specs=[pl.BlockSpec(memory_space=pltpu.VMEM)],
        out_specs=pl.BlockSpec(memory_space=pltpu.HBM),
        out_shape=pltpu.HBM(shape, src.dtype),
        scratch_shapes=[pltpu.SemaphoreType.DMA((replicas,))],
        compiler_params=params(8),
        cost_estimate=cost(SPREAD_FLOPS, 2 * src.size * (replicas + 1)),
        name="spread_rows",
    )(src)


def shift(value, axis, by):
    n = lax.axis_size(axis)
    return lax.ppermute(value, axis, [(i, (i + by) % n) for i in range(n)])


def swap_cores(value):
    return lax.ppermute(value, "c", [(0, 1), (1, 0)])


def ring_gather(value, axis):
    return [value] + [shift(value, axis, -k) for k in (1, 2, 3)]


def slot_ranks(owner_row):
    positions = jnp.arange(owner_row.shape[0])
    same_owner = owner_row[:, None] == owner_row[None, :]
    earlier = positions[None, :] < positions[:, None]
    return jnp.sum(jnp.where(same_owner & earlier, 1, 0), axis=1).astype(jnp.int32)


def body(activations, out_grads, owners, left_stats, right_stats, left_roots, right_roots):
    tokens, own_blocks, order = out_grads.shape
    replicas = lax.axis_size("y") * lax.axis_size("x")
    planes, cores = lax.axis_size("z"), lax.axis_size("c")
    strip = order // replicas
    slots = left_stats.shape[1]
    cols = activations.shape[1]

    owner_row = owners[0, :, 0]
    where = owner_row * slots + slot_ranks(owner_row)
    count = jnp.sum(jnp.where(owner_row == lax.axis_index(DP), 1, 0)).astype(jnp.int32).reshape(1)

    turned = out_grads.reshape(tokens, own_blocks, replicas, strip).transpose(2, 1, 3, 0)
    turned = turned.reshape(replicas, own_blocks * strip, tokens)
    own = lax.all_to_all(turned, DP, 0, 0, tiled=True)
    spread = spread_rows(activations, replicas)
    own, spread = lax.optimization_barrier((own, spread))
    acts = lax.all_to_all(spread, DP, 0, 0, tiled=True)

    down, up = shift(own, "z", 1), shift(own, "z", -1)
    own_too = swap_cores(own)
    h = replicas // 2
    far_lo, far_hi = shift(down[:h], "z", 1), shift(up[h:], "z", -1)
    down_too, up_too = swap_cores(down), swap_cores(up)
    far_lo_too, far_hi_too = swap_cores(far_lo), swap_cores(far_hi)
    pieces = [own, own_too, down, down_too, up, up_too, far_lo, far_hi, far_lo_too, far_hi_too]

    z, c = lax.axis_index("z"), lax.axis_index("c")
    zs = [z, (z + planes - 1) % planes, (z + 1) % planes, (z + 2) % planes]
    first = jnp.stack([(q * cores + k) * own_blocks for q in zs for k in (c, 1 - c)]).astype(jnp.int32)
    strips = grad_strips(where, first, acts.reshape(replicas * tokens, cols), pieces, replicas * slots, strip)
    early = jnp.where(lax.axis_index("c") == 1, jnp.minimum(count, EARLY_SLOTS), 0)
    lroots, rroots, _ = lax.optimization_barrier((left_roots[0], right_roots[0], strips))
    fours = root_powers(early, lroots, rroots)
    strips, *fours = lax.optimization_barrier((strips, *fours))
    arrived = lax.all_to_all(strips.reshape(replicas, slots, strip, cols), DP, 0, 0, tiled=True)
    lroots, rroots, _ = lax.optimization_barrier((left_roots[0], right_roots[0], strips))
    late = root_powers(count, lroots, rroots)
    from_early = (jnp.arange(slots) < early[0])[:, None, None]
    lfour, rfour = (jnp.where(from_early, f, t) for f, t in zip(fours, late))
    arrived, lfour, rfour = lax.optimization_barrier((arrived, lfour, rfour))
    ready = directions(count, arrived, left_roots[0], right_roots[0])
    returned = lax.all_to_all(ready, DP, 0, 0, tiled=True)
    nls, nrs, nlr, nrr = update_slots(
        count, arrived, left_stats[0], right_stats[0], left_roots[0], right_roots[0], lfour, rfour
    )
    direction = pick(where, returned.reshape(replicas * slots, strip, cols))
    return nls[None], nrs[None], nlr[None], nrr[None], direction


def solution(mesh):
    fsdp, dp = mesh.shape["fsdp"], mesh.shape["dp"]
    torus = Mesh(mesh.devices.reshape(fsdp // 2, 2, dp // 4, 4), ("z", "c", "y", "x"))
    state = P(FSDP, DP, None, None)
    in_specs = (P(DP, FSDP), P(DP, FSDP, None), P(FSDP, None, None), state, state, state, state)
    out_specs = (state, state, state, state, P(None, DP, FSDP))
    return jax.shard_map(body, mesh=torus, in_specs=in_specs, out_specs=out_specs, check_vma=False)
```
